512 devices in a mesh: pairs: 32 (over y, x), aux: 16 (over z, core).
Axes of the slice: x: 4, y: 8, z: 8, core: 2. Of those that a mesh axis runs over, the one named last changes fastest.
Arguments:
- factors: bfloat16 [4096, 2048, 128], P('aux', 'pairs'), may hold values from -1 to 1
- coefficients: bfloat16 [2048, 256, 128], P(('pairs', 'aux')), may hold values from -0.375 to 0.375
- amplitudes: bfloat16 [2048, 128, 128], P(('pairs', 'aux')), may hold values from -6 to 6
- domains: int32 [2048, 256], P(('pairs', 'aux')), may hold values from 0 to 4413, as said below
- partners: int32 [2048, 12], P(('pairs', 'aux')), may hold values from 0 to 2047, as said below
- couplings: float32 [2048, 12], P(('pairs', 'aux')), may hold values from -4 to 4
- energies: float32 [2048, 128], P(('pairs', 'aux')), may hold values from 0.5 to 4
Outputs:
- residual: float32 [2048, 128, 128], P(('pairs', 'aux'))
The draws below stay inside these ranges and needn't reach their ends.
Inputs may be any that keep to these rules, and one draw needn't show every extreme that they name: `partners`: row p names 12 different pairs other than p, all within the run of 65 consecutive pair numbers centred on p, moved inward where it would pass 0 or 2047. `domains`: each row holds 256 different function numbers.
All inputs are finite; a program needn't handle non-finite values.
Results may differ from the reference program's by a relative error of at most 0.0065.
Values may be sent and summed in bfloat16 or wider, within the bound.
A program may use at most 128 MiB of HBM per device.

```python
import math
import jax
import jax.numpy as jnp
from jax import lax

NCPL = 12
NPNO = 128
DOM = 256
NAUX = 4096
PAIRS = 2048
SPAN = 32
AUX_SLAB = 256
N_AUX = 16


def draw_partners(key, part):
    reach_pairs = SPAN
    pair_ids = jnp.arange(PAIRS, dtype=jnp.int32)
    starts = jnp.clip(pair_ids - reach_pairs, 0, PAIRS - 1 - 2 * reach_pairs)
    offsets = jnp.arange(2 * reach_pairs + 1, dtype=jnp.int32)
    scores = jax.random.randint(jax.random.fold_in(key, 11), (PAIRS, 2 * reach_pairs + 1), 0, 1 << 20, dtype=jnp.int32)
    scores = scores * 1024 + offsets[None, :]
    scores = jnp.where(offsets[None, :] == (pair_ids - starts)[:, None], 2147483647, scores)
    order = jnp.argsort(scores, axis=1, stable=True).astype(jnp.int32)
    return (starts[:, None] + order[:, :NCPL]).astype(jnp.int32)


def draw_domains(key, part):
    step_size = DOM // 128
    window_len = DOM + DOM // 4
    pair_ids = jnp.arange(PAIRS, dtype=jnp.int32)
    starts = pair_ids * step_size
    offsets = jnp.arange(window_len, dtype=jnp.int32)
    scores = jax.random.randint(jax.random.fold_in(key, 23), (PAIRS, window_len), 0, 1 << 20, dtype=jnp.int32)
    scores = scores * 1024 + offsets[None, :]
    order = jnp.argsort(scores, axis=1, stable=True).astype(jnp.int32)
    return (starts[:, None] + order[:, :DOM]).astype(jnp.int32)


def draw_factors(key, part):
    slab_count = NAUX // AUX_SLAB
    identity = jnp.eye(NPNO, dtype=jnp.float32)
    total_scale = 8.0
    level_reach = 1.1
    mean_power = (math.exp(2.0 * level_reach) - math.exp(-2.0 * level_reach)) / (4.0 * level_reach)
    row_scale = math.sqrt(total_scale / (NAUX * mean_power))

    def one_pair(pair_id):
        pair_key = jax.random.fold_in(jax.random.fold_in(key, 31), pair_id)
        noise_key = jax.random.fold_in(pair_key, 1)
        mix_key = jax.random.fold_in(pair_key, 2)
        level_key = jax.random.fold_in(pair_key, 3)
        own_mix = jax.random.normal(mix_key, (NPNO, NPNO), jnp.float32)
        noise = jnp.clip(jax.random.normal(noise_key, (NAUX, NPNO), jnp.float32), -5.0, 5.0)
        mixing = identity + own_mix / math.sqrt(NPNO)
        levels = jax.random.uniform(level_key, (slab_count,), jnp.float32, -level_reach, level_reach)
        slab_weights = jnp.repeat(jnp.exp(levels), AUX_SLAB)
        rows = jnp.dot(noise, mixing, precision=lax.Precision.HIGHEST)
        rows = rows * (slab_weights * row_scale)[:, None]
        return jnp.clip(rows, -1.0, 1.0).astype(jnp.bfloat16)
    stacked = lax.map(one_pair, jnp.arange(PAIRS, dtype=jnp.int32))
    return jnp.transpose(stacked, (1, 0, 2))


def shard_levels(stream_key, extent, shards, least, top_value):
    def one(axis_at, parts):
        heights = jax.random.uniform(jax.random.fold_in(jax.random.fold_in(stream_key, 6), axis_at), (parts,), jnp.float32, least / len(shards), top_value / len(shards))
        return jnp.repeat(jnp.exp(heights), extent[axis_at] // parts).reshape((-1,) + (1,) * (len(extent) - axis_at - 1))

    gain = one(*shards[0])
    for cut in shards[1:]:
        gain = gain * one(*cut)
    return gain


def bell_draw(own_key, extent, deviation, most, cuts=(), kind=jnp.bfloat16):
    result = jax.random.normal(own_key, extent, jnp.float32) * deviation
    if len(cuts) > 0:
        result = shard_levels(own_key, extent, cuts, -0.22, 0.18) * result
    return jnp.clip(result, min=-most, max=most).astype(kind)


def setup_inputs(seed: int = 0) -> dict:
    splits = jax.random.split(jax.random.key(seed), 8)
    factors = draw_factors(jax.random.fold_in(splits[7], 71), 0)
    coefficients = bell_draw(splits[1], (PAIRS, DOM, NPNO), DOM ** -0.5, 0.375, ((0, 512),))
    amplitudes = bell_draw(splits[2], (PAIRS, NPNO, NPNO), 1.0, 6.0, ((0, 512),))
    domains = draw_domains(jax.random.fold_in(splits[7], 71), 0)
    partners = draw_partners(jax.random.fold_in(splits[7], 71), 0)
    couplings = bell_draw(splits[5], (PAIRS, NCPL), 1.0, 4.0, ((0, 512),), jnp.float32)
    energies = jnp.clip(jnp.exp(math.log(4.0) - 2.0794415 * jax.random.uniform(splits[6], (PAIRS, NPNO), jnp.float32) ** shard_levels(splits[6], (PAIRS, NPNO), ((0, 512),), -0.2, 0.2)), 0.5, 4.0)
    return {"factors": factors, "coefficients": coefficients, "amplitudes": amplitudes, "domains": domains, "partners": partners, "couplings": couplings, "energies": energies}


def reference(factors, coefficients, amplitudes, domains, partners, couplings, energies):
    def per_pair(pair_id):
        aux_column = lax.dynamic_index_in_dim(factors, pair_id, 1, keepdims=False)
        slab_rows = aux_column.astype(jnp.float32).reshape(N_AUX, NAUX // N_AUX, NPNO)
        slab_terms = jnp.einsum("sxa,sxb->sab", slab_rows, slab_rows, precision=lax.Precision.HIGHEST)
        slab_terms = lax.optimization_barrier(slab_terms.astype(jnp.bfloat16)).astype(jnp.float32)
        exchange_k = jnp.sum(slab_terms, axis=0)
        listed = partners[pair_id]
        own_coeff = coefficients[pair_id]
        own_funcs = domains[pair_id]
        far_coeff = coefficients[listed]
        far_amps = amplitudes[listed]
        far_funcs = domains[listed]
        same_func = own_funcs[None, :, None] == far_funcs[:, None, :]
        has_match = jnp.any(same_func, axis=2)
        position = jnp.sum(jnp.where(same_func, jnp.arange(DOM, dtype=jnp.int32)[None, None, :], 0), axis=2, dtype=jnp.int32).astype(jnp.int32)
        picked = jax.vmap(lambda rows, where_rows: rows[where_rows])(far_coeff, position)
        matched = jnp.where(has_match[:, :, None], picked, jnp.zeros((), jnp.bfloat16))
        intersection = jnp.einsum("fa,cfn->can", own_coeff.astype(jnp.float32), matched.astype(jnp.float32), precision=lax.Precision.HIGHEST).astype(jnp.bfloat16)
        mixed_rows = jnp.einsum("can,cnm->cam", intersection.astype(jnp.float32), far_amps.astype(jnp.float32), precision=lax.Precision.HIGHEST).astype(jnp.bfloat16)
        coupled = jnp.einsum("cam,cbm->cab", mixed_rows.astype(jnp.float32), intersection.astype(jnp.float32), precision=lax.Precision.HIGHEST)
        cycle_term = jnp.sum(couplings[pair_id][:, None, None] * coupled, axis=0)
        pair_energy = energies[pair_id]
        diagonal_term = (pair_energy[:, None] + pair_energy[None, :]) * amplitudes[pair_id].astype(jnp.float32)
        return exchange_k + diagonal_term - cycle_term

    return lax.map(per_pair, jnp.arange(PAIRS, dtype=jnp.int32))
```

```python
import functools

import jax
import jax.numpy as jnp
from jax import lax
from jax.experimental import pallas as pl
from jax.experimental.pallas import tpu as pltpu
from jax.sharding import PartitionSpec as P

MESH = pl.DeviceIdType.MESH
F32 = jnp.float32
BF16 = jnp.bfloat16

REACH = 4
BLOCKS = 2 * REACH + 1
CHUNKS = 2
PACKED = 272


def packed_rows(squares):
    row = lax.broadcasted_iota(jnp.int32, (64, 128), 0)
    lane = lax.broadcasted_iota(jnp.int32, (64, 128), 1)
    parts, diagonals = [], []
    for square in squares:
        low = pltpu.roll(square[64:], 64, 1)
        parts.append(jnp.where(lane < row, low, square[:64]))
        diagonals.append(jnp.sum(jnp.where(lane == row, low, 0.0), axis=0, keepdims=True))
    return parts, jnp.concatenate(diagonals + [jnp.zeros((12, 128), F32)], axis=0)


def unpacked(part, diagonal):
    row = lax.broadcasted_iota(jnp.int32, (64, 128), 0)
    lane = lax.broadcasted_iota(jnp.int32, (64, 128), 1)
    upper = jnp.where(lane > row, part, 0.0)
    lower = pltpu.roll(jnp.where(lane < row, part, 0.0), 64, 1)
    strict = jnp.concatenate([upper, lower], axis=0)
    first = jnp.where(lane == row, part, 0.0)
    second = jnp.where(lane == row + 64, pltpu.roll(jnp.broadcast_to(diagonal, (8, 128)), 64, 1)[:1], 0.0)
    return strict + strict.T + jnp.concatenate([first, second], axis=0)


def kernel(
    pairs_count,
    fac, coef, amp, dom, prt, cpl, eng,
    out,
    cw, tw, dw, fbuf, wide, slab_own, slab_out, slab_in, up_out, up_in, down_out, down_in, inter, mixed,
    own_sem, fac_sem,
    c_send, c_recv, t_send, t_recv, d_send, d_recv,
    cs_send, cs_recv, ts_send, ts_recv, ds_send, ds_recv,
    far_send, slab_send, slab_recv, up_send, up_recv, down_send, down_recv,
):
    aux = lax.axis_index("aux")
    me = lax.axis_index("pairs") * 16 + aux
    total = pairs_count * 16
    chip = me // 2
    chips = total // 2
    core = lax.rem(aux, 2)
    z = aux // 2
    other = me + 1 - 2 * core
    column = me - aux
    above = column + lax.rem(aux + 2, 16)
    below = column + lax.rem(aux + 14, 16)
    has_up = me + 2 < total
    has_down = me >= 2
    feeds_first = (chip > REACH) & (chip <= 2 * REACH)
    feeds_last = (chip >= chips - 1 - 2 * REACH) & (chip < chips - 1 - REACH)
    is_first = chip == 0
    is_last = chip == chips - 1
    goes = (has_up, has_down)

    def place(d):
        d = lax.rem(d + total, total)
        return {"pairs": d // 16, "aux": lax.rem(d, 16)}

    barrier = pltpu.get_barrier_semaphore()

    def greet(d):
        pl.semaphore_signal(barrier, inc=1, device_id=place(d), device_id_type=MESH)

    greet(other)
    greet(above)
    greet(below)

    @pl.when((z == 7) & has_up)
    def _():
        greet(me + 2)

    @pl.when((z == 0) & has_down)
    def _():
        greet(me - 2)

    @pl.when(feeds_first)
    def _():
        greet(core)

    @pl.when(feeds_last)
    def _():
        greet(total - 2 + core)

    @pl.when(is_first)
    def _():
        for s in range(1, REACH + 1):
            greet(2 * (2 * REACH + 1 - s) + core)

    @pl.when(is_last)
    def _():
        for s in range(1, REACH + 1):
            greet(2 * (chips - 2 - 2 * REACH + s) + core)

    one = lambda flag: flag.astype(jnp.int32)
    pl.semaphore_wait(
        barrier,
        3
        + one((z == 7) & has_up)
        + one((z == 0) & has_down)
        + one(feeds_first)
        + one(feeds_last)
        + REACH * (one(is_first) + one(is_last)),
    )

    def piece(k, slot, c):
        if k < CHUNKS:
            return cw.at[pl.ds(slot * 8 + c * 4 + k * 2, 2)]
        if k == CHUNKS:
            return tw.at[pl.ds(slot * 8 + c * 4, 4)]
        return dw.at[slot * 2 + c]

    def source(k):
        if k < CHUNKS:
            return coef.at[pl.ds(k * 2, 2)]
        if k == CHUNKS:
            return amp
        return dom

    sends = (c_send, c_send, t_send, d_send)
    recvs = (c_recv, c_recv, t_recv, d_recv)
    sib_sends = (cs_send, cs_send, ts_send, ds_send)
    sib_recvs = (cs_recv, cs_recv, ts_recv, ds_recv)
    C0, C1, T, D = 0, 1, 2, 3

    def at_slot(dr, s):
        return REACH - s if dr == 0 else REACH + s

    def ring(dr, s, k):
        src = source(k) if s == 1 else piece(k, at_slot(dr, s - 1), core)
        return pltpu.make_async_remote_copy(
            src, piece(k, at_slot(dr, s), core),
            sends[k].at[dr, s - 1, k % 2], recvs[k].at[dr, s - 1, k % 2],
            device_id=place(me + 2 if dr == 0 else me - 2), device_id_type=MESH,
        )

    def ring_start(dr, s, k):
        @pl.when(goes[dr])
        def _():
            ring(dr, s, k).start()

    def to_sibling(slot, k):
        src = source(k) if slot == REACH else piece(k, slot, core)
        return pltpu.make_async_remote_copy(
            src, piece(k, slot, core),
            sib_sends[k].at[slot, k % 2], sib_recvs[k].at[slot, k % 2],
            device_id=place(other), device_id_type=MESH,
        )

    def to_first(k):
        slot = chip - (REACH + 1)
        return pltpu.make_async_remote_copy(
            source(k), piece(k, slot, core),
            far_send.at[0, k], recvs[k].at[0, REACH - 1 - slot, k % 2],
            device_id=place(core), device_id_type=MESH,
        )

    def to_last(k):
        s = chip - (chips - 2 - 2 * REACH)
        return pltpu.make_async_remote_copy(
            source(k), piece(k, REACH + s, core),
            far_send.at[1, k], recvs[k].at[1, s - 1, k % 2],
            device_id=place(total - 2 + core), device_id_type=MESH,
        )

    def own(k):
        return pltpu.make_async_copy(source(k), piece(k, REACH, core), own_sem.at[k])

    def begin(k):
        for dr in range(2):
            ring_start(dr, 1, k)

        @pl.when(feeds_first)
        def _():
            to_first(k).start()

        @pl.when(feeds_last)
        def _():
            to_last(k).start()

    def arrive(dr, s, k):
        ring_recv(dr, s, k)
        if s < REACH:
            ring_start(dr, s + 1, k)
        to_sibling(at_slot(dr, s), k).start()

    def ring_recv(dr, s, k):
        ring(dr, s, k).wait_recv()

    def column_of(k):
        off = jnp.where(lax.rem(k, 2) == 0, 4 - k // 2, k // 2 - 3)
        return lax.rem(z + off + 8, 8)

    def fac_copy(k):
        return pltpu.make_async_copy(
            fac.at[:, pl.ds(pl.multiple_of(column_of(k) * 8, 8), 8), :], fbuf.at[k], fac_sem.at[k]
        )

    for k in (D, C0, C1):
        begin(k)
    for k in range(8):
        fac_copy(k).start()
    for k in (D, C0, C1, T):
        own(k).start()
        to_sibling(REACH, k).start()

    def slab_to_sibling(k):
        return pltpu.make_async_remote_copy(
            slab_out.at[k], slab_in.at[k], slab_send.at[k], slab_recv.at[k],
            device_id=place(other), device_id_type=MESH,
        )

    def slab_group(k, carry):
        fac_copy(k).wait()
        wide[...] = fbuf[k].astype(F32).reshape(2048, 128)
        squares = []
        for j in range(8):
            rows = wide[pl.ds(j, 256, stride=8), :].astype(BF16)
            squares.append(
                lax.dot_general(rows, rows, (((0,), (0,)), ((), ())), preferred_element_type=F32)
            )
        halves = [packed_rows(squares[:4]), packed_rows(squares[4:])]

        def put(ref, half):
            parts, diagonals = half
            for i, part in enumerate(parts):
                ref[k, pl.ds(i * 64, 64), :] = part.astype(BF16)
            ref[k, pl.ds(256, 16), :] = diagonals.astype(BF16)

        @pl.when(core == 0)
        def _():
            put(slab_own, halves[0])
            put(slab_out, halves[1])

        @pl.when(core == 1)
        def _():
            put(slab_own, halves[1])
            put(slab_out, halves[0])

        slab_to_sibling(k).start()
        return carry

    def chip_sum(k):
        slab_to_sibling(k).wait_recv()
        return slab_own[k].astype(F32) + slab_in[k].astype(F32)

    def up_copy(r):
        return pltpu.make_async_remote_copy(
            up_out.at[r], up_in.at[r], up_send.at[r], up_recv.at[r],
            device_id=place(above), device_id_type=MESH,
        )

    def down_copy(r):
        return pltpu.make_async_remote_copy(
            down_out.at[r], down_in.at[r], down_send.at[r], down_recv.at[r],
            device_id=place(below), device_id_type=MESH,
        )

    def sum_step(r):
        value = chip_sum(2 * r)
        if r > 0:
            up_copy(r - 1).wait_recv()
            value = value + up_in[r - 1].astype(F32)
        up_out[r] = value.astype(BF16)
        up_copy(r).start()
        if r < 3:
            value = chip_sum(2 * r + 1)
            if r > 0:
                down_copy(r - 1).wait_recv()
                value = value + down_in[r - 1].astype(F32)
            down_out[r] = value.astype(BF16)
            down_copy(r).start()

    lax.fori_loop(0, 4, slab_group, 0)
    for dr in range(2):
        arrive(dr, 1, D)
        arrive(dr, 1, C0)
    lax.fori_loop(4, 8, slab_group, 0)
    sum_step(0)
    for dr in range(2):
        arrive(dr, 1, C1)
    for s in range(2, REACH + 1):
        for dr in range(2):
            arrive(dr, s, D)
            arrive(dr, s, C0)
        sum_step(s - 1)
        if s == REACH:
            begin(T)
        for dr in range(2):
            arrive(dr, s, C1)

    up_copy(3).wait_recv()
    down_copy(2).wait_recv()
    summed = chip_sum(7) + up_in[3].astype(F32) + down_in[2].astype(F32)
    for j in range(4):
        out[j] = unpacked(summed[j * 64 : (j + 1) * 64], summed[256 + j : 257 + j])

    for k in (D, C0, C1):
        own(k).wait()
        for slot in range(BLOCKS):
            to_sibling(slot, k).wait_recv()

    def slot_of(q):
        apart = q // 8 - chip
        apart = jnp.where(apart > REACH, apart - BLOCKS, apart)
        apart = jnp.where(apart < -REACH, apart + BLOCKS, apart)
        return jnp.clip(apart + REACH, 0, BLOCKS - 1) * 8 + lax.rem(q, 8)

    def intersect(p):
        mine = cw[REACH * 8 + core * 4 + p]
        mine_t = mine.T
        rows = dw[REACH * 2 + core]
        funcs = jnp.broadcast_to(rows[p : p + 1], (128, 256)).T
        funcs = jnp.concatenate([funcs, funcs], axis=1)
        for c in range(12):
            slot = slot_of(prt[p, c])
            theirs = dw[slot // 4, pl.ds(lax.rem(slot, 4), 1), :]
            same = (funcs == theirs).astype(F32).astype(BF16)
            spread = jnp.dot(mine_t, same, preferred_element_type=F32).astype(BF16)
            inter[p, :, c * 128 : (c + 1) * 128] = jnp.dot(
                spread, cw[slot], preferred_element_type=F32
            ).astype(BF16)

    for p in range(4):
        intersect(p)
        for dr in range(2):
            arrive(dr, p + 1, T)

    own(T).wait()
    for slot in range(BLOCKS):
        to_sibling(slot, T).wait_recv()

    for p in range(4):
        for c in range(12):
            slot = slot_of(prt[p, c])
            part = jnp.dot(inter[p, :, c * 128 : (c + 1) * 128], tw[slot], preferred_element_type=F32)
            mixed[:, c * 128 : (c + 1) * 128] = (part * cpl[p, c]).astype(BF16)
        cycle = lax.dot_general(
            mixed[...], inter[p], (((1,), (1,)), ((), ())), preferred_element_type=F32
        )
        level = jnp.broadcast_to(eng[p : p + 1, :], (128, 128))
        own_amp = tw[REACH * 8 + core * 4 + p].astype(F32)
        out[p] = out[p] + (level + level.T) * own_amp - cycle

    for k in (D, C0, C1, T):
        for dr in range(2):
            @pl.when(goes[dr])
            def _():
                for s in range(1, REACH + 1):
                    ring(dr, s, k).wait_send()
        for slot in range(BLOCKS):
            to_sibling(slot, k).wait_send()

        @pl.when(feeds_first)
        def _():
            to_first(k).wait_send()

        @pl.when(feeds_last)
        def _():
            to_last(k).wait_send()

    for k in range(8):
        slab_to_sibling(k).wait_send()
    for r in range(4):
        up_copy(r).wait_send()
    for r in range(3):
        down_copy(r).wait_send()


def solution(mesh):
    pairs_count = mesh.shape["pairs"]
    dma = pltpu.SemaphoreType.DMA
    whole = pl.BlockSpec(memory_space=pltpu.VMEM)
    any_space = pl.BlockSpec(memory_space=pl.ANY)
    smem = pl.BlockSpec(memory_space=pltpu.SMEM)
    block = (PACKED, 128)
    call = pl.pallas_call(
        functools.partial(kernel, pairs_count),
        out_shape=jax.ShapeDtypeStruct((4, 128, 128), F32),
        in_specs=[any_space, any_space, any_space, any_space, smem, smem, whole],
        out_specs=whole,
        scratch_shapes=[
            pltpu.VMEM((BLOCKS * 8, 256, 128), BF16),
            pltpu.VMEM((BLOCKS * 8, 128, 128), BF16),
            pltpu.VMEM((BLOCKS * 2, 4, 256), jnp.int32),
            pltpu.VMEM((8, 256, 8, 128), BF16),
            pltpu.VMEM((2048, 128), F32),
            pltpu.VMEM((8,) + block, BF16),
            pltpu.VMEM((8,) + block, BF16),
            pltpu.VMEM((8,) + block, BF16),
            pltpu.VMEM((4,) + block, BF16),
            pltpu.VMEM((4,) + block, BF16),
            pltpu.VMEM((3,) + block, BF16),
            pltpu.VMEM((3,) + block, BF16),
            pltpu.VMEM((4, 128, 1536), BF16),
            pltpu.VMEM((128, 1536), BF16),
            dma((4,)),
            dma((8,)),
        ]
        + [dma((2, REACH, 2))] * 6
        + [dma((BLOCKS, 2))] * 6
        + [dma((2, 4)), dma((8,)), dma((8,)), dma((4,)), dma((4,)), dma((3,)), dma((3,))],
        compiler_params=pltpu.CompilerParams(
            collective_id=0, has_side_effects=True, vmem_limit_bytes=48 << 20
        ),
    )
    split = P(("pairs", "aux"), None)
    cube = P(("pairs", "aux"), None, None)
    return jax.shard_map(
        call,
        mesh=mesh,
        in_specs=(P("aux", "pairs", None), cube, cube, split, split, split, split),
        out_specs=cube,
        check_vma=False,
    )
```

```python
import functools

import jax
import jax.numpy as jnp
from jax import lax
from jax.experimental import pallas as pl
from jax.experimental.pallas import tpu as pltpu
from jax.sharding import PartitionSpec as P

MESH = pl.DeviceIdType.MESH
F32 = jnp.float32
BF16 = jnp.bfloat16

REACH = 4
BLOCKS = 2 * REACH + 1
PACKED = 272


def packed_rows(squares):
    row = lax.broadcasted_iota(jnp.int32, (64, 128), 0)
    lane = lax.broadcasted_iota(jnp.int32, (64, 128), 1)
    parts, diagonals = [], []
    for square in squares:
        low = pltpu.roll(square[64:], 64, 1)
        parts.append(jnp.where(lane < row, low, square[:64]))
        diagonals.append(jnp.sum(jnp.where(lane == row, low, 0.0), axis=0, keepdims=True))
    return parts, jnp.concatenate(diagonals + [jnp.zeros((12, 128), F32)], axis=0)


def unpacked(part, diagonal):
    row = lax.broadcasted_iota(jnp.int32, (64, 128), 0)
    lane = lax.broadcasted_iota(jnp.int32, (64, 128), 1)
    upper = jnp.where(lane > row, part, 0.0)
    lower = pltpu.roll(jnp.where(lane < row, part, 0.0), 64, 1)
    strict = jnp.concatenate([upper, lower], axis=0)
    first = jnp.where(lane == row, part, 0.0)
    second = jnp.where(lane == row + 64, pltpu.roll(jnp.broadcast_to(diagonal, (8, 128)), 64, 1)[:1], 0.0)
    return strict + strict.T + jnp.concatenate([first, second], axis=0)


def kernel(
    pairs_count,
    fac, coef, amp, dom, prt_hbm, cpl_hbm, eng_hbm,
    out,
    cw, tw, dw, prt, cpl, eng, fbuf, wide, slab_own, slab_out, slab_in, up_out, up_in, down_out, down_in, inter, mixed,
    own_sem, fac_sem, small_sem,
    ring_send, ring_recv, sib_send, sib_recv, far_send,
    slab_send, slab_recv, up_send, up_recv, down_send, down_recv,
):
    aux = lax.axis_index("aux")
    me = lax.axis_index("pairs") * 16 + aux
    total = pairs_count * 16
    chip = me // 2
    chips = total // 2
    core = lax.rem(aux, 2)
    z = aux // 2
    other = me + 1 - 2 * core
    column = me - aux
    above = column + lax.rem(aux + 2, 16)
    below = column + lax.rem(aux + 14, 16)
    goes = (me + 2 < total, me >= 2)
    reach = (me + 2, me - 2)
    feeds = (chip == 2 * REACH, chip == chips - 1 - 2 * REACH)
    ends = (core, total - 2 + core)
    is_end = (chip == 0, chip == chips - 1)
    feeders = (4 * REACH + core, total - 2 - 4 * REACH + core)

    def place(d):
        d = lax.rem(d + total, total)
        return {"pairs": d // 16, "aux": lax.rem(d, 16)}

    barrier = pltpu.get_barrier_semaphore()
    greeted = jnp.int32(0)
    for flag, d in (
        (None, other), (None, above), (None, below),
        ((z == 7) & goes[0], reach[0]), ((z == 0) & goes[1], reach[1]),
        (feeds[0], ends[0]), (feeds[1], ends[1]), (is_end[0], feeders[0]), (is_end[1], feeders[1]),
    ):
        def greet(d=d):
            pl.semaphore_signal(barrier, inc=1, device_id=place(d), device_id_type=MESH)

        if flag is None:
            greet()
            greeted = greeted + 1
        else:
            pl.when(flag)(greet)
            greeted = greeted + flag.astype(jnp.int32)
    pl.semaphore_wait(barrier, greeted)

    def piece(kind, k, slot, c):
        if kind == "C":
            return cw.at[slot * 8 + c * 4 + k]
        if kind == "T":
            return tw.at[pl.ds(slot * 8 + c * 4 + k * 2, 2)]
        return dw.at[slot * 2 + c]

    def source(kind, k):
        if kind == "C":
            return coef.at[k]
        if kind == "T":
            return amp.at[pl.ds(k * 2, 2)]
        return dom

    def mark(kind, k):
        return k + {"C": 0, "T": 4, "D": 6}[kind]

    def at_slot(dr, s):
        return REACH - s if dr == 0 else REACH + s

    def hop(dr, s, kind, k, first, to, send_sem):
        src = source(kind, k) if first else piece(kind, k, at_slot(dr, s - 1), core)
        return pltpu.make_async_remote_copy(
            src, piece(kind, k, at_slot(dr, s), core), send_sem, ring_recv.at[dr, s - 1, mark(kind, k)],
            device_id=place(to), device_id_type=MESH,
        )

    def ring(dr, s, kind, k, first=False):
        return hop(dr, s, kind, k, first, reach[dr], ring_send.at[dr, s - 1, mark(kind, k)])

    def far(dr, s, kind, k, first=False):
        return hop(dr, s, kind, k, first, ends[dr], far_send.at[s - 1, mark(kind, k)])

    def pass_on(dr, s, kind, k, first=False):
        @pl.when(goes[dr])
        def _():
            ring(dr, s, kind, k, first).start()

        @pl.when(feeds[dr])
        def _():
            far(dr, s, kind, k, first).start()

    def to_sibling(slot, kind, k, first=False):
        src = source(kind, k) if first else piece(kind, k, slot, core)
        m = mark(kind, k)
        return pltpu.make_async_remote_copy(
            src, piece(kind, k, slot, core), sib_send.at[slot, m], sib_recv.at[slot, m],
            device_id=place(other), device_id_type=MESH,
        )

    def own(kind, k):
        return pltpu.make_async_copy(source(kind, k), piece(kind, k, REACH, core), own_sem.at[mark(kind, k)])

    def begin(kind, k):
        for dr in range(2):
            pass_on(dr, 1, kind, k, True)

    def arrive(s, kind, k, last=False):
        for dr in range(2):
            ring(dr, s, kind, k).wait_recv()
            if not last:
                pass_on(dr, s + 1, kind, k)
            to_sibling(at_slot(dr, s), kind, k).start()

    pieces = [("D", 0)] + [("C", k) for k in range(4)] + [("T", k) for k in range(2)]

    def column_of(k):
        off = jnp.where(lax.rem(k, 2) == 0, 4 - k // 2, k // 2 - 3)
        return lax.rem(z + off + 8, 8)

    def fac_copy(k):
        return pltpu.make_async_copy(
            fac.at[:, pl.ds(pl.multiple_of(column_of(k) * 8, 8), 8), :], fbuf.at[k], fac_sem.at[k]
        )

    smalls = [
        pltpu.make_async_copy(src, dst, small_sem.at[i])
        for i, (src, dst) in enumerate(((prt_hbm, prt), (cpl_hbm, cpl), (eng_hbm, eng)))
    ]

    for kind, k in pieces[:5]:
        begin(kind, k)
    lax.fori_loop(0, 8, lambda k, carry: (fac_copy(k).start(), carry)[1], 0)
    for kind, k in pieces:
        own(kind, k).start()
        to_sibling(REACH, kind, k, True).start()
    for copy in smalls:
        copy.start()

    def slab_to_sibling(k):
        return pltpu.make_async_remote_copy(
            slab_out.at[k], slab_in.at[k], slab_send.at[k], slab_recv.at[k],
            device_id=place(other), device_id_type=MESH,
        )

    def slab_group(k):
        fac_copy(k).wait()
        wide[...] = fbuf[k].astype(F32).reshape(2048, 128)
        squares = []
        for j in range(8):
            rows = wide[pl.ds(j, 256, stride=8), :].astype(BF16)
            squares.append(
                lax.dot_general(rows, rows, (((0,), (0,)), ((), ())), preferred_element_type=F32)
            )
        halves = [packed_rows(squares[:4]), packed_rows(squares[4:])]

        def put(ref, half):
            parts, diagonals = half
            for i, part in enumerate(parts):
                ref[k, pl.ds(i * 64, 64), :] = part.astype(BF16)
            ref[k, pl.ds(256, 16), :] = diagonals.astype(BF16)

        @pl.when(core == 0)
        def _():
            put(slab_own, halves[0])
            put(slab_out, halves[1])

        @pl.when(core == 1)
        def _():
            put(slab_own, halves[1])
            put(slab_out, halves[0])

        slab_to_sibling(k).start()

    def chip_sum(k):
        slab_to_sibling(k).wait_recv()
        return slab_own[k].astype(F32) + slab_in[k].astype(F32)

    def up_copy(r):
        return pltpu.make_async_remote_copy(
            up_out.at[r], up_in.at[r], up_send.at[r], up_recv.at[r],
            device_id=place(above), device_id_type=MESH,
        )

    def down_copy(r):
        return pltpu.make_async_remote_copy(
            down_out.at[r], down_in.at[r], down_send.at[r], down_recv.at[r],
            device_id=place(below), device_id_type=MESH,
        )

    def sum_step(r):
        value = chip_sum(2 * r)
        if r > 0:
            up_copy(r - 1).wait_recv()
            value = value + up_in[r - 1].astype(F32)
        up_out[r] = value.astype(BF16)
        up_copy(r).start()
        if r < 3:
            value = chip_sum(2 * r + 1)
            if r > 0:
                down_copy(r - 1).wait_recv()
                value = value + down_in[r - 1].astype(F32)
            down_out[r] = value.astype(BF16)
            down_copy(r).start()

    def loop(low, high):
        def run(body):
            def step(i, carry):
                body(i)
                return carry

            lax.fori_loop(low, high, step, 0)

        return run

    @loop(0, 4)
    def _(i):
        slab_group(i)
        arrive(1, "C", i)

    arrive(1, "D", 0)
    for k in range(2):
        begin("T", k)
    @loop(0, 4)
    def _(i):
        slab_group(4 + i)
        arrive(2, "C", i)

    arrive(2, "D", 0)
    for k in range(2):
        arrive(1, "T", k)
    sum_step(0)

    @loop(0, 4)
    def _(i):
        arrive(3, "C", i)

    arrive(3, "D", 0)
    for k in range(2):
        arrive(2, "T", k)
    sum_step(1)

    @loop(0, 4)
    def _(i):
        arrive(4, "C", i, True)

    arrive(4, "D", 0, True)
    sum_step(2)

    for copy in smalls:
        copy.wait()
    for kind, k in pieces[:5]:
        own(kind, k).wait()

    @loop(0, BLOCKS)
    def _(slot):
        for kind, k in pieces[:5]:
            to_sibling(slot, kind, k).wait_recv()

    def slot_of(q):
        apart = q // 8 - chip
        apart = jnp.where(apart > REACH, apart - BLOCKS, apart)
        apart = jnp.where(apart < -REACH, apart + BLOCKS, apart)
        return jnp.clip(apart + REACH, 0, BLOCKS - 1) * 8 + lax.rem(q, 8)

    def intersect(p):
        mine_t = cw[REACH * 8 + core * 4 + p].T
        funcs = jnp.broadcast_to(dw[REACH * 2 + core, pl.ds(p, 1), :], (128, 256)).T
        funcs = jnp.concatenate([funcs, funcs], axis=1)
        for c in range(12):
            slot = slot_of(prt[p, c])
            theirs = dw[slot // 4, pl.ds(lax.rem(slot, 4), 1), :]
            same = (funcs == theirs).astype(F32).astype(BF16)
            spread = jnp.dot(mine_t, same, preferred_element_type=F32).astype(BF16)
            inter[p, :, c * 128 : (c + 1) * 128] = jnp.dot(
                spread, cw[slot], preferred_element_type=F32
            ).astype(BF16)

    @loop(0, 2)
    def _(i):
        intersect(i)
        arrive(3, "T", i)

    @loop(0, 2)
    def _(i):
        intersect(2 + i)
        arrive(4, "T", i, True)

    sum_step(3)
    for k in range(2):
        own("T", k).wait()

    @loop(0, BLOCKS)
    def _(slot):
        for kind, k in pieces[5:]:
            to_sibling(slot, kind, k).wait_recv()

    for p in range(4):
        for c in range(12):
            slot = slot_of(prt[p, c])
            part = jnp.dot(inter[p, :, c * 128 : (c + 1) * 128], tw[slot], preferred_element_type=F32)
            mixed[:, c * 128 : (c + 1) * 128] = (part * cpl[p, c]).astype(BF16)
        cycle = lax.dot_general(
            mixed[...], inter[p], (((1,), (1,)), ((), ())), preferred_element_type=F32
        )
        level = jnp.broadcast_to(eng[p : p + 1, :], (128, 128))
        own_amp = tw[REACH * 8 + core * 4 + p].astype(F32)
        out[p] = (level + level.T) * own_amp - cycle

    up_copy(3).wait_recv()
    down_copy(2).wait_recv()
    summed = chip_sum(7) + up_in[3].astype(F32) + down_in[2].astype(F32)
    for p in range(4):
        out[p] = out[p] + unpacked(summed[p * 64 : (p + 1) * 64], summed[256 + p : 257 + p])


    for dr in range(2):
        for test, copy in ((goes[dr], ring), (feeds[dr], far)):
            @pl.when(test)
            def _():
                @loop(1, REACH + 1)
                def _(s):
                    for kind, k in pieces:
                        copy(dr, s, kind, k).wait_send()

    @loop(0, BLOCKS)
    def _(slot):
        for kind, k in pieces:
            to_sibling(slot, kind, k).wait_send()

    for k in range(8):
        slab_to_sibling(k).wait_send()
    for r in range(4):
        up_copy(r).wait_send()
    for r in range(3):
        down_copy(r).wait_send()


def solution(mesh):
    pairs_count = mesh.shape["pairs"]
    dma = pltpu.SemaphoreType.DMA
    whole = pl.BlockSpec(memory_space=pltpu.VMEM)
    hbm = pl.BlockSpec(memory_space=pltpu.HBM)
    block = (PACKED, 128)
    call = pl.pallas_call(
        functools.partial(kernel, pairs_count),
        out_shape=jax.ShapeDtypeStruct((4, 128, 128), F32),
        in_specs=[hbm] * 7,
        out_specs=whole,
        scratch_shapes=[
            pltpu.VMEM((BLOCKS * 8, 256, 128), BF16),
            pltpu.VMEM((BLOCKS * 8, 128, 128), BF16),
            pltpu.VMEM((BLOCKS * 2, 4, 256), jnp.int32),
            pltpu.SMEM((4, 12), jnp.int32),
            pltpu.SMEM((4, 12), F32),
            pltpu.VMEM((4, 128), F32),
            pltpu.VMEM((8, 256, 8, 128), BF16),
            pltpu.VMEM((2048, 128), F32),
            pltpu.VMEM((8,) + block, BF16),
            pltpu.VMEM((8,) + block, BF16),
            pltpu.VMEM((8,) + block, BF16),
            pltpu.VMEM((4,) + block, BF16),
            pltpu.VMEM((4,) + block, BF16),
            pltpu.VMEM((3,) + block, BF16),
            pltpu.VMEM((3,) + block, BF16),
            pltpu.VMEM((4, 128, 1536), BF16),
            pltpu.VMEM((128, 1536), BF16),
            dma((7,)),
            dma((8,)),
            dma((3,)),
            dma((2, REACH, 7)),
            dma((2, REACH, 7)),
            dma((BLOCKS, 7)),
            dma((BLOCKS, 7)),
            dma((REACH, 7)),
            dma((8,)),
            dma((8,)),
            dma((4,)),
            dma((4,)),
            dma((3,)),
            dma((3,)),
        ],
        compiler_params=pltpu.CompilerParams(
            collective_id=0, has_side_effects=True, vmem_limit_bytes=58 << 20
        ),
    )
    split = P(("pairs", "aux"), None)
    cube = P(("pairs", "aux"), None, None)
    return jax.shard_map(
        call,
        mesh=mesh,
        in_specs=(P("aux", "pairs", None), cube, cube, split, split, split, split),
        out_specs=cube,
        check_vma=False,
    )
```

```python
import functools

import jax
import jax.numpy as jnp
from jax import lax
from jax.experimental import pallas as pl
from jax.experimental.pallas import tpu as pltpu
from jax.sharding import PartitionSpec as P

MESH = pl.DeviceIdType.MESH
F32 = jnp.float32
BF16 = jnp.bfloat16

REACH = 4
BLOCKS = 2 * REACH + 1
PACKED = 272


def packed_rows(squares):
    row = lax.broadcasted_iota(jnp.int32, (64, 128), 0)
    lane = lax.broadcasted_iota(jnp.int32, (64, 128), 1)
    parts, diagonals = [], []
    for square in squares:
        low = pltpu.roll(square[64:], 64, 1)
        parts.append(jnp.where(lane < row, low, square[:64]))
        diagonals.append(jnp.sum(jnp.where(lane == row, low, 0.0), axis=0, keepdims=True))
    return parts, jnp.concatenate(diagonals + [jnp.zeros((12, 128), F32)], axis=0)


def unpacked(part, diagonal):
    row = lax.broadcasted_iota(jnp.int32, (64, 128), 0)
    lane = lax.broadcasted_iota(jnp.int32, (64, 128), 1)
    upper = jnp.where(lane > row, part, 0.0)
    lower = pltpu.roll(jnp.where(lane < row, part, 0.0), 64, 1)
    strict = jnp.concatenate([upper, lower], axis=0)
    first = jnp.where(lane == row, part, 0.0)
    second = jnp.where(lane == row + 64, pltpu.roll(jnp.broadcast_to(diagonal, (8, 128)), 64, 1)[:1], 0.0)
    return strict + strict.T + jnp.concatenate([first, second], axis=0)


def kernel(
    pairs_count,
    fac, coef, amp, dom, prt_hbm, cpl_hbm, eng_hbm,
    out,
    cw, tw, dw, prt, cpl, eng, fbuf, wide, slab_own, slab_out, slab_in, up_out, up_in, down_out, down_in, inter, mixed,
    own_sem, fac_sem, small_sem,
    ring_send, ring_recv, sib_send, sib_recv, far_send,
    slab_send, slab_recv, up_send, up_recv, down_send, down_recv,
):
    aux = lax.axis_index("aux")
    me = lax.axis_index("pairs") * 16 + aux
    total = pairs_count * 16
    chip = me // 2
    chips = total // 2
    core = lax.rem(aux, 2)
    z = aux // 2
    other = me + 1 - 2 * core
    column = me - aux
    above = column + lax.rem(aux + 2, 16)
    below = column + lax.rem(aux + 14, 16)
    goes = (me + 2 < total, me >= 2)
    reach = (me + 2, me - 2)
    feeds = (chip == 2 * REACH, chip == chips - 1 - 2 * REACH)
    ends = (core, total - 2 + core)
    is_end = (chip == 0, chip == chips - 1)
    feeders = (4 * REACH + core, total - 2 - 4 * REACH + core)

    def place(d):
        d = lax.rem(d + total, total)
        return {"pairs": d // 16, "aux": lax.rem(d, 16)}

    barrier = pltpu.get_barrier_semaphore()
    greeted = jnp.int32(0)
    for flag, d in (
        (None, other), (None, above), (None, below),
        ((z == 7) & goes[0], reach[0]), ((z == 0) & goes[1], reach[1]),
        (feeds[0], ends[0]), (feeds[1], ends[1]), (is_end[0], feeders[0]), (is_end[1], feeders[1]),
    ):
        def greet(d=d):
            pl.semaphore_signal(barrier, inc=1, device_id=place(d), device_id_type=MESH)

        if flag is None:
            greet()
            greeted = greeted + 1
        else:
            pl.when(flag)(greet)
            greeted = greeted + flag.astype(jnp.int32)
    pl.semaphore_wait(barrier, greeted)

    def piece(kind, k, slot, c):
        if kind == "C":
            return cw.at[slot * 8 + c * 4 + k]
        if kind == "T":
            return tw.at[pl.ds(slot * 8 + c * 4 + k * 2, 2)]
        return dw.at[slot * 2 + c]

    def source(kind, k):
        if kind == "C":
            return coef.at[k]
        if kind == "T":
            return amp.at[pl.ds(k * 2, 2)]
        return dom

    def mark(kind, k):
        return k + {"C": 0, "T": 4, "D": 6}[kind]

    def at_slot(dr, s):
        return REACH - s if dr == 0 else REACH + s

    def hop(dr, s, kind, k, first, to, send_sem):
        src = source(kind, k) if first else piece(kind, k, at_slot(dr, s - 1), core)
        return pltpu.make_async_remote_copy(
            src, piece(kind, k, at_slot(dr, s), core), send_sem, ring_recv.at[dr, s - 1, mark(kind, k)],
            device_id=place(to), device_id_type=MESH,
        )

    def ring(dr, s, kind, k, first=False):
        return hop(dr, s, kind, k, first, reach[dr], ring_send.at[dr, s - 1, mark(kind, k)])

    def far(dr, s, kind, k, first=False):
        return hop(dr, s, kind, k, first, ends[dr], far_send.at[s - 1, mark(kind, k)])

    def pass_on(dr, s, kind, k, first=False):
        @pl.when(goes[dr])
        def _():
            ring(dr, s, kind, k, first).start()

        @pl.when(feeds[dr])
        def _():
            far(dr, s, kind, k, first).start()

    def to_sibling(slot, kind, k, first=False):
        src = source(kind, k) if first else piece(kind, k, slot, core)
        m = mark(kind, k)
        return pltpu.make_async_remote_copy(
            src, piece(kind, k, slot, core), sib_send.at[slot, m], sib_recv.at[slot, m],
            device_id=place(other), device_id_type=MESH,
        )

    def own(kind, k):
        return pltpu.make_async_copy(source(kind, k), piece(kind, k, REACH, core), own_sem.at[mark(kind, k)])

    def begin(kind, k):
        for dr in range(2):
            pass_on(dr, 1, kind, k, True)

    def arrive(s, kind, k, last=False):
        for dr in range(2):
            ring(dr, s, kind, k).wait_recv()
            if not last:
                pass_on(dr, s + 1, kind, k)
            to_sibling(at_slot(dr, s), kind, k).start()

    pieces = [("D", 0)] + [("C", k) for k in range(4)] + [("T", k) for k in range(2)]

    def column_of(k):
        off = jnp.where(lax.rem(k, 2) == 0, 4 - k // 2, k // 2 - 3)
        return lax.rem(z + off + 8, 8)

    def fac_copy(k):
        return pltpu.make_async_copy(
            fac.at[:, pl.ds(pl.multiple_of(column_of(k) * 8, 8), 8), :], fbuf.at[k], fac_sem.at[k]
        )

    smalls = [
        pltpu.make_async_copy(src, dst, small_sem.at[i])
        for i, (src, dst) in enumerate(((prt_hbm, prt), (cpl_hbm, cpl), (eng_hbm, eng)))
    ]

    for kind, k in pieces[:5]:
        begin(kind, k)
    lax.fori_loop(0, 8, lambda k, carry: (fac_copy(k).start(), carry)[1], 0)
    for kind, k in pieces:
        own(kind, k).start()
        to_sibling(REACH, kind, k, True).start()
    for copy in smalls:
        copy.start()

    def slab_to_sibling(k):
        return pltpu.make_async_remote_copy(
            slab_out.at[k], slab_in.at[k], slab_send.at[k], slab_recv.at[k],
            device_id=place(other), device_id_type=MESH,
        )

    def slab_group(k):
        fac_copy(k).wait()
        wide[...] = fbuf[k].astype(F32).reshape(2048, 128)
        squares = []
        for j in range(8):
            rows = wide[pl.ds(j, 256, stride=8), :].astype(BF16)
            squares.append(
                lax.dot_general(rows, rows, (((0,), (0,)), ((), ())), preferred_element_type=F32)
            )
        halves = [packed_rows(squares[:4]), packed_rows(squares[4:])]

        def put(ref, half):
            parts, diagonals = half
            for i, part in enumerate(parts):
                ref[k, pl.ds(i * 64, 64), :] = part.astype(BF16)
            ref[k, pl.ds(256, 16), :] = diagonals.astype(BF16)

        @pl.when(core == 0)
        def _():
            put(slab_own, halves[0])
            put(slab_out, halves[1])

        @pl.when(core == 1)
        def _():
            put(slab_own, halves[1])
            put(slab_out, halves[0])

        slab_to_sibling(k).start()

    def chip_sum(k):
        slab_to_sibling(k).wait_recv()
        return slab_own[k].astype(F32) + slab_in[k].astype(F32)

    halves_of = (pl.ds(0, 144), pl.ds(144, 128))
    stage_blocks = ((0, 2, 4, 6), (0, 1, 3, 5))

    def sum_copy(dr, r):
        outgoing, incoming, send, recv, to = (
            (up_out, up_in, up_send, up_recv, above),
            (down_out, down_in, down_send, down_recv, below),
        )[dr]
        rows = halves_of[dr] if r == 0 else pl.ds(0, PACKED)
        return pltpu.make_async_remote_copy(
            outgoing.at[r, rows], incoming.at[r, rows], send.at[r], recv.at[r],
            device_id=place(to), device_id_type=MESH,
        )

    def sum_step(r):
        opposite = chip_sum(0) if r == 0 else None
        for dr, outgoing, incoming in ((0, up_out, up_in), (1, down_out, down_in)):
            if r == 0:
                rows = halves_of[dr]
                outgoing[0, rows, :] = opposite[rows.start : rows.start + rows.size].astype(BF16)
            else:
                value = chip_sum(stage_blocks[dr][r])
                sum_copy(dr, r - 1).wait_recv()
                if r > 1:
                    outgoing[r] = (value + incoming[r - 1].astype(F32)).astype(BF16)
                else:
                    rows, rest = halves_of[dr], halves_of[1 - dr]
                    met = value[rows.start : rows.start + rows.size] + incoming[0, rows, :].astype(F32)
                    outgoing[1, rows, :] = met.astype(BF16)
                    outgoing[1, rest, :] = value[rest.start : rest.start + rest.size].astype(BF16)
            sum_copy(dr, r).start()

    def loop(low, high):
        def run(body):
            def step(i, carry):
                body(i)
                return carry

            lax.fori_loop(low, high, step, 0)

        return run

    @loop(0, 4)
    def _(i):
        slab_group(i)
        arrive(1, "C", i)

    arrive(1, "D", 0)
    for k in range(2):
        begin("T", k)
    @loop(0, 4)
    def _(i):
        slab_group(4 + i)
        arrive(2, "C", i)

    arrive(2, "D", 0)
    for k in range(2):
        arrive(1, "T", k)
    sum_step(0)

    @loop(0, 4)
    def _(i):
        arrive(3, "C", i)

    arrive(3, "D", 0)
    for k in range(2):
        arrive(2, "T", k)
    sum_step(1)

    @loop(0, 4)
    def _(i):
        arrive(4, "C", i, True)

    arrive(4, "D", 0, True)
    sum_step(2)

    for copy in smalls:
        copy.wait()
    for kind, k in pieces[:5]:
        own(kind, k).wait()

    @loop(0, BLOCKS)
    def _(slot):
        for kind, k in pieces[:5]:
            to_sibling(slot, kind, k).wait_recv()

    def slot_of(q):
        apart = q // 8 - chip
        apart = jnp.where(apart > REACH, apart - BLOCKS, apart)
        apart = jnp.where(apart < -REACH, apart + BLOCKS, apart)
        return jnp.clip(apart + REACH, 0, BLOCKS - 1) * 8 + lax.rem(q, 8)

    def intersect(p):
        mine_t = cw[REACH * 8 + core * 4 + p].T
        funcs = jnp.broadcast_to(dw[REACH * 2 + core, pl.ds(p, 1), :], (128, 256)).T
        funcs = jnp.concatenate([funcs, funcs], axis=1)
        for c in range(12):
            slot = slot_of(prt[p, c])
            theirs = dw[slot // 4, pl.ds(lax.rem(slot, 4), 1), :]
            same = (funcs == theirs).astype(F32).astype(BF16)
            spread = jnp.dot(mine_t, same, preferred_element_type=F32).astype(BF16)
            inter[p, :, c * 128 : (c + 1) * 128] = jnp.dot(
                spread, cw[slot], preferred_element_type=F32
            ).astype(BF16)

    @loop(0, 2)
    def _(i):
        intersect(i)
        arrive(3, "T", i)

    sum_step(3)

    @loop(0, 2)
    def _(i):
        intersect(2 + i)
        arrive(4, "T", i, True)

    for k in range(2):
        own("T", k).wait()

    @loop(0, BLOCKS)
    def _(slot):
        for kind, k in pieces[5:]:
            to_sibling(slot, kind, k).wait_recv()

    for p in range(4):
        for c in range(12):
            slot = slot_of(prt[p, c])
            part = jnp.dot(inter[p, :, c * 128 : (c + 1) * 128], tw[slot], preferred_element_type=F32)
            mixed[:, c * 128 : (c + 1) * 128] = (part * cpl[p, c]).astype(BF16)
        cycle = lax.dot_general(
            mixed[...], inter[p], (((1,), (1,)), ((), ())), preferred_element_type=F32
        )
        level = jnp.broadcast_to(eng[p : p + 1, :], (128, 128))
        own_amp = tw[REACH * 8 + core * 4 + p].astype(F32)
        out[p] = (level + level.T) * own_amp - cycle

    for dr in range(2):
        sum_copy(dr, 3).wait_recv()
    summed = chip_sum(7) + up_in[3].astype(F32) + down_in[3].astype(F32)
    for p in range(4):
        out[p] = out[p] + unpacked(summed[p * 64 : (p + 1) * 64], summed[256 + p : 257 + p])


    for dr in range(2):
        for test, copy in ((goes[dr], ring), (feeds[dr], far)):
            @pl.when(test)
            def _():
                @loop(1, REACH + 1)
                def _(s):
                    for kind, k in pieces:
                        copy(dr, s, kind, k).wait_send()

    @loop(0, BLOCKS)
    def _(slot):
        for kind, k in pieces:
            to_sibling(slot, kind, k).wait_send()

    for k in range(8):
        slab_to_sibling(k).wait_send()
    for r in range(4):
        for dr in range(2):
            sum_copy(dr, r).wait_send()


def solution(mesh):
    pairs_count = mesh.shape["pairs"]
    dma = pltpu.SemaphoreType.DMA
    whole = pl.BlockSpec(memory_space=pltpu.VMEM)
    hbm = pl.BlockSpec(memory_space=pltpu.HBM)
    block = (PACKED, 128)
    call = pl.pallas_call(
        functools.partial(kernel, pairs_count),
        out_shape=jax.ShapeDtypeStruct((4, 128, 128), F32),
        in_specs=[hbm] * 7,
        out_specs=whole,
        scratch_shapes=[
            pltpu.VMEM((BLOCKS * 8, 256, 128), BF16),
            pltpu.VMEM((BLOCKS * 8, 128, 128), BF16),
            pltpu.VMEM((BLOCKS * 2, 4, 256), jnp.int32),
            pltpu.SMEM((4, 12), jnp.int32),
            pltpu.SMEM((4, 12), F32),
            pltpu.VMEM((4, 128), F32),
            pltpu.VMEM((8, 256, 8, 128), BF16),
            pltpu.VMEM((2048, 128), F32),
            pltpu.VMEM((8,) + block, BF16),
            pltpu.VMEM((8,) + block, BF16),
            pltpu.VMEM((8,) + block, BF16),
            pltpu.VMEM((4,) + block, BF16),
            pltpu.VMEM((4,) + block, BF16),
            pltpu.VMEM((4,) + block, BF16),
            pltpu.VMEM((4,) + block, BF16),
            pltpu.VMEM((4, 128, 1536), BF16),
            pltpu.VMEM((128, 1536), BF16),
            dma((7,)),
            dma((8,)),
            dma((3,)),
            dma((2, REACH, 7)),
            dma((2, REACH, 7)),
            dma((BLOCKS, 7)),
            dma((BLOCKS, 7)),
            dma((REACH, 7)),
            dma((8,)),
            dma((8,)),
            dma((4,)),
            dma((4,)),
            dma((4,)),
            dma((4,)),
        ],
        compiler_params=pltpu.CompilerParams(
            collective_id=0, has_side_effects=True, vmem_limit_bytes=58 << 20
        ),
    )
    split = P(("pairs", "aux"), None)
    cube = P(("pairs", "aux"), None, None)
    return jax.shard_map(
        call,
        mesh=mesh,
        in_specs=(P("aux", "pairs", None), cube, cube, split, split, split, split),
        out_specs=cube,
        check_vma=False,
    )
```

```python
import functools

import jax
import jax.numpy as jnp
from jax import lax
from jax.experimental import pallas as pl
from jax.experimental.pallas import tpu as pltpu
from jax.sharding import PartitionSpec as P

MESH = pl.DeviceIdType.MESH
F32 = jnp.float32
BF16 = jnp.bfloat16

REACH = 4
BLOCKS = 2 * REACH + 1
PACKED = 272


def packed_rows(squares):
    row = lax.broadcasted_iota(jnp.int32, (64, 128), 0)
    lane = lax.broadcasted_iota(jnp.int32, (64, 128), 1)
    parts, diagonals = [], []
    for square in squares:
        low = pltpu.roll(square[64:], 64, 1)
        parts.append(jnp.where(lane < row, low, square[:64]))
        diagonals.append(jnp.sum(jnp.where(lane == row, low, 0.0), axis=0, keepdims=True))
    return parts, jnp.concatenate(diagonals + [jnp.zeros((12, 128), F32)], axis=0)


def unpacked(part, diagonal):
    row = lax.broadcasted_iota(jnp.int32, (64, 128), 0)
    lane = lax.broadcasted_iota(jnp.int32, (64, 128), 1)
    upper = jnp.where(lane > row, part, 0.0)
    lower = pltpu.roll(jnp.where(lane < row, part, 0.0), 64, 1)
    strict = jnp.concatenate([upper, lower], axis=0)
    first = jnp.where(lane == row, part, 0.0)
    second = jnp.where(lane == row + 64, pltpu.roll(jnp.broadcast_to(diagonal, (8, 128)), 64, 1)[:1], 0.0)
    return strict + strict.T + jnp.concatenate([first, second], axis=0)


def kernel(
    pairs_count,
    fac, coef, amp, dom, prt_hbm, cpl_hbm, eng_hbm,
    out,
    cw, tw, dw, prt, cpl, eng, fbuf, wide, slab_own, slab_out, slab_in, up_out, up_in, down_out, down_in, inter, mixed,
    own_sem, fac_sem, small_sem,
    ring_send, ring_recv, sib_send, sib_recv, far_send,
    slab_send, slab_recv, up_send, up_recv, down_send, down_recv,
):
    aux = lax.axis_index("aux")
    me = lax.axis_index("pairs") * 16 + aux
    total = pairs_count * 16
    chip = me // 2
    chips = total // 2
    core = lax.rem(aux, 2)
    z = aux // 2
    other = me + 1 - 2 * core
    column = me - aux
    above = column + lax.rem(aux + 2, 16)
    below = column + lax.rem(aux + 14, 16)
    goes = (me + 2 < total, me >= 2)
    reach = (me + 2, me - 2)
    feeds = (chip == 2 * REACH, chip == chips - 1 - 2 * REACH)
    ends = (core, total - 2 + core)
    is_end = (chip == 0, chip == chips - 1)
    feeders = (4 * REACH + core, total - 2 - 4 * REACH + core)

    def place(d):
        d = lax.rem(d + total, total)
        return {"pairs": d // 16, "aux": lax.rem(d, 16)}

    barrier = pltpu.get_barrier_semaphore()
    greeted = jnp.int32(0)
    for flag, d in (
        (None, other), (None, above), (None, below),
        ((z == 7) & goes[0], reach[0]), ((z == 0) & goes[1], reach[1]),
        (feeds[0], ends[0]), (feeds[1], ends[1]), (is_end[0], feeders[0]), (is_end[1], feeders[1]),
    ):
        def greet(d=d):
            pl.semaphore_signal(barrier, inc=1, device_id=place(d), device_id_type=MESH)

        if flag is None:
            greet()
            greeted = greeted + 1
        else:
            pl.when(flag)(greet)
            greeted = greeted + flag.astype(jnp.int32)
    pl.semaphore_wait(barrier, greeted)

    def piece(kind, k, slot, c):
        if kind == "C":
            return cw.at[slot * 8 + c * 4 + k]
        if kind == "T":
            return tw.at[pl.ds(slot * 8 + c * 4 + k * 2, 2)]
        return dw.at[slot * 2 + c]

    def source(kind, k):
        if kind == "C":
            return coef.at[k]
        if kind == "T":
            return amp.at[pl.ds(k * 2, 2)]
        return dom

    def mark(kind, k):
        return k + {"C": 0, "T": 4, "D": 6}[kind]

    def at_slot(dr, s):
        return REACH - s if dr == 0 else REACH + s

    def hop(dr, s, kind, k, first, to, send_sem):
        src = source(kind, k) if first else piece(kind, k, at_slot(dr, s - 1), core)
        return pltpu.make_async_remote_copy(
            src, piece(kind, k, at_slot(dr, s), core), send_sem, ring_recv.at[dr, s - 1, mark(kind, k)],
            device_id=place(to), device_id_type=MESH,
        )

    def ring(dr, s, kind, k, first=False):
        return hop(dr, s, kind, k, first, reach[dr], ring_send.at[dr, s - 1, mark(kind, k)])

    def far(dr, s, kind, k, first=False):
        return hop(dr, s, kind, k, first, ends[dr], far_send.at[s - 1, mark(kind, k)])

    def pass_on(dr, s, kind, k, first=False):
        @pl.when(goes[dr])
        def _():
            ring(dr, s, kind, k, first).start()

        @pl.when(feeds[dr])
        def _():
            far(dr, s, kind, k, first).start()

    def to_sibling(slot, kind, k, first=False):
        src = source(kind, k) if first else piece(kind, k, slot, core)
        m = mark(kind, k)
        return pltpu.make_async_remote_copy(
            src, piece(kind, k, slot, core), sib_send.at[slot, m], sib_recv.at[slot, m],
            device_id=place(other), device_id_type=MESH,
        )

    def own(kind, k):
        return pltpu.make_async_copy(source(kind, k), piece(kind, k, REACH, core), own_sem.at[mark(kind, k)])

    def begin(kind, k):
        for dr in range(2):
            pass_on(dr, 1, kind, k, True)

    def arrive(s, kind, k, last=False):
        for dr in range(2):
            ring(dr, s, kind, k).wait_recv()
            if not last:
                pass_on(dr, s + 1, kind, k)
            to_sibling(at_slot(dr, s), kind, k).start()

    pieces = [("D", 0)] + [("C", k) for k in range(4)] + [("T", k) for k in range(2)]

    def column_of(k):
        off = jnp.where(lax.rem(k, 2) == 0, 4 - k // 2, k // 2 - 3)
        return lax.rem(z + off + 8, 8)

    def fac_copy(k):
        return pltpu.make_async_copy(
            fac.at[:, pl.ds(pl.multiple_of(column_of(k) * 8, 8), 8), :], fbuf.at[k], fac_sem.at[k]
        )

    smalls = [
        pltpu.make_async_copy(src, dst, small_sem.at[i])
        for i, (src, dst) in enumerate(((prt_hbm, prt), (cpl_hbm, cpl), (eng_hbm, eng)))
    ]

    for kind, k in pieces[:5]:
        begin(kind, k)
    lax.fori_loop(0, 8, lambda k, carry: (fac_copy(k).start(), carry)[1], 0)
    for kind, k in pieces:
        own(kind, k).start()
        to_sibling(REACH, kind, k, True).start()
    for copy in smalls:
        copy.start()

    def slab_to_sibling(k):
        return pltpu.make_async_remote_copy(
            slab_out.at[k], slab_in.at[k], slab_send.at[k], slab_recv.at[k],
            device_id=place(other), device_id_type=MESH,
        )

    def slab_group(k):
        fac_copy(k).wait()
        wide[...] = fbuf[k].astype(F32).reshape(2048, 128)
        squares = []
        for j in range(8):
            rows = wide[pl.ds(j, 256, stride=8), :].astype(BF16)
            squares.append(
                lax.dot_general(rows, rows, (((0,), (0,)), ((), ())), preferred_element_type=F32)
            )
        halves = [packed_rows(squares[:4]), packed_rows(squares[4:])]

        def put(ref, half):
            parts, diagonals = half
            for i, part in enumerate(parts):
                ref[k, pl.ds(i * 64, 64), :] = part.astype(BF16)
            ref[k, pl.ds(256, 16), :] = diagonals.astype(BF16)

        @pl.when(core == 0)
        def _():
            put(slab_own, halves[0])
            put(slab_out, halves[1])

        @pl.when(core == 1)
        def _():
            put(slab_own, halves[1])
            put(slab_out, halves[0])

        slab_to_sibling(k).start()

    def chip_sum(k):
        slab_to_sibling(k).wait_recv()
        return slab_own[k].astype(F32) + slab_in[k].astype(F32)

    halves_of = (pl.ds(0, 144), pl.ds(144, 128))
    stage_blocks = ((0, 2, 4, 6), (0, 1, 3, 5))

    def sum_copy(dr, r):
        outgoing, incoming, send, recv, to = (
            (up_out, up_in, up_send, up_recv, above),
            (down_out, down_in, down_send, down_recv, below),
        )[dr]
        rows = halves_of[dr] if r == 0 else pl.ds(0, PACKED)
        return pltpu.make_async_remote_copy(
            outgoing.at[r, rows], incoming.at[r, rows], send.at[r], recv.at[r],
            device_id=place(to), device_id_type=MESH,
        )

    def sum_step(r):
        opposite = chip_sum(0) if r == 0 else None
        for dr, outgoing, incoming in ((0, up_out, up_in), (1, down_out, down_in)):
            if r == 0:
                rows = halves_of[dr]
                outgoing[0, rows, :] = opposite[rows.start : rows.start + rows.size].astype(BF16)
            else:
                value = chip_sum(stage_blocks[dr][r])
                sum_copy(dr, r - 1).wait_recv()
                if r > 1:
                    outgoing[r] = (value + incoming[r - 1].astype(F32)).astype(BF16)
                else:
                    rows, rest = halves_of[dr], halves_of[1 - dr]
                    met = value[rows.start : rows.start + rows.size] + incoming[0, rows, :].astype(F32)
                    outgoing[1, rows, :] = met.astype(BF16)
                    outgoing[1, rest, :] = value[rest.start : rest.start + rest.size].astype(BF16)
            sum_copy(dr, r).start()

    def loop(low, high):
        def run(body):
            def step(i, carry):
                body(i)
                return carry

            lax.fori_loop(low, high, step, 0)

        return run

    @loop(0, 4)
    def _(i):
        slab_group(i)
        arrive(1, "C", i)

    arrive(1, "D", 0)
    for k in range(2):
        begin("T", k)
    @loop(0, 4)
    def _(i):
        slab_group(4 + i)
        arrive(2, "C", i)

    arrive(2, "D", 0)
    for k in range(2):
        arrive(1, "T", k)
    sum_step(0)

    @loop(0, 4)
    def _(i):
        arrive(3, "C", i)

    arrive(3, "D", 0)
    for k in range(2):
        arrive(2, "T", k)
    sum_step(1)

    @loop(0, 4)
    def _(i):
        arrive(4, "C", i, True)

    arrive(4, "D", 0, True)
    sum_step(2)

    for copy in smalls:
        copy.wait()
    for kind, k in pieces[:5]:
        own(kind, k).wait()

    @loop(0, BLOCKS)
    def _(slot):
        for kind, k in pieces[:5]:
            to_sibling(slot, kind, k).wait_recv()

    def slot_of(q):
        apart = q // 8 - chip
        apart = jnp.where(apart > REACH, apart - BLOCKS, apart)
        apart = jnp.where(apart < -REACH, apart + BLOCKS, apart)
        return jnp.clip(apart + REACH, 0, BLOCKS - 1) * 8 + lax.rem(q, 8)

    def intersect(p):
        mine_t = cw[REACH * 8 + core * 4 + p].T
        funcs = jnp.broadcast_to(dw[REACH * 2 + core, pl.ds(p, 1), :], (128, 256)).T
        funcs = jnp.concatenate([funcs, funcs], axis=1)
        for c in range(12):
            slot = slot_of(prt[p, c])
            theirs = dw[slot // 4, pl.ds(lax.rem(slot, 4), 1), :]
            same = (funcs == theirs).astype(F32).astype(BF16)
            spread = jnp.dot(mine_t, same, preferred_element_type=F32).astype(BF16)
            inter[p, :, c * 128 : (c + 1) * 128] = jnp.dot(
                spread, cw[slot], preferred_element_type=F32
            ).astype(BF16)

    @loop(0, 2)
    def _(i):
        intersect(i)
        arrive(3, "T", i)

    intersect(2)
    arrive(4, "T", 0, True)
    sum_step(3)
    intersect(3)
    arrive(4, "T", 1, True)

    for k in range(2):
        own("T", k).wait()

    @loop(0, BLOCKS)
    def _(slot):
        for kind, k in pieces[5:]:
            to_sibling(slot, kind, k).wait_recv()

    for p in range(4):
        for c in range(12):
            slot = slot_of(prt[p, c])
            part = jnp.dot(inter[p, :, c * 128 : (c + 1) * 128], tw[slot], preferred_element_type=F32)
            mixed[:, c * 128 : (c + 1) * 128] = (part * cpl[p, c]).astype(BF16)
        cycle = lax.dot_general(
            mixed[...], inter[p], (((1,), (1,)), ((), ())), preferred_element_type=F32
        )
        level = jnp.broadcast_to(eng[p : p + 1, :], (128, 128))
        own_amp = tw[REACH * 8 + core * 4 + p].astype(F32)
        out[p] = (level + level.T) * own_amp - cycle

    for dr in range(2):
        sum_copy(dr, 3).wait_recv()
    summed = chip_sum(7) + up_in[3].astype(F32) + down_in[3].astype(F32)
    for p in range(4):
        out[p] = out[p] + unpacked(summed[p * 64 : (p + 1) * 64], summed[256 + p : 257 + p])


    for dr in range(2):
        for test, copy in ((goes[dr], ring), (feeds[dr], far)):
            @pl.when(test)
            def _():
                @loop(1, REACH + 1)
                def _(s):
                    for kind, k in pieces:
                        copy(dr, s, kind, k).wait_send()

    @loop(0, BLOCKS)
    def _(slot):
        for kind, k in pieces:
            to_sibling(slot, kind, k).wait_send()

    for k in range(8):
        slab_to_sibling(k).wait_send()
    for r in range(4):
        for dr in range(2):
            sum_copy(dr, r).wait_send()


def solution(mesh):
    pairs_count = mesh.shape["pairs"]
    dma = pltpu.SemaphoreType.DMA
    whole = pl.BlockSpec(memory_space=pltpu.VMEM)
    hbm = pl.BlockSpec(memory_space=pltpu.HBM)
    block = (PACKED, 128)
    call = pl.pallas_call(
        functools.partial(kernel, pairs_count),
        out_shape=jax.ShapeDtypeStruct((4, 128, 128), F32),
        in_specs=[hbm] * 7,
        out_specs=whole,
        scratch_shapes=[
            pltpu.VMEM((BLOCKS * 8, 256, 128), BF16),
            pltpu.VMEM((BLOCKS * 8, 128, 128), BF16),
            pltpu.VMEM((BLOCKS * 2, 4, 256), jnp.int32),
            pltpu.SMEM((4, 12), jnp.int32),
            pltpu.SMEM((4, 12), F32),
            pltpu.VMEM((4, 128), F32),
            pltpu.VMEM((8, 256, 8, 128), BF16),
            pltpu.VMEM((2048, 128), F32),
            pltpu.VMEM((8,) + block, BF16),
            pltpu.VMEM((8,) + block, BF16),
            pltpu.VMEM((8,) + block, BF16),
            pltpu.VMEM((4,) + block, BF16),
            pltpu.VMEM((4,) + block, BF16),
            pltpu.VMEM((4,) + block, BF16),
            pltpu.VMEM((4,) + block, BF16),
            pltpu.VMEM((4, 128, 1536), BF16),
            pltpu.VMEM((128, 1536), BF16),
            dma((7,)),
            dma((8,)),
            dma((3,)),
            dma((2, REACH, 7)),
            dma((2, REACH, 7)),
            dma((BLOCKS, 7)),
            dma((BLOCKS, 7)),
            dma((REACH, 7)),
            dma((8,)),
            dma((8,)),
            dma((4,)),
            dma((4,)),
            dma((4,)),
            dma((4,)),
        ],
        compiler_params=pltpu.CompilerParams(
            collective_id=0, has_side_effects=True, vmem_limit_bytes=58 << 20
        ),
    )
    split = P(("pairs", "aux"), None)
    cube = P(("pairs", "aux"), None, None)
    return jax.shard_map(
        call,
        mesh=mesh,
        in_specs=(P("aux", "pairs", None), cube, cube, split, split, split, split),
        out_specs=cube,
        check_vma=False,
    )
```
